512 devices in a mesh: ctx: 64 (over z, y), tp: 8 (over x, core).
Axes of the slice: x: 4, y: 8, z: 8, core: 2. Of those that a mesh axis runs over, the one named last changes fastest.
Arguments:
- queries: bfloat16 [32768, 5120], P('ctx', 'tp'), may hold values from -150 to 150
- keys_values: bfloat16 [2, 32768, 1024], P(None, 'ctx', 'tp'), may hold values from -6 to 6
- doc_lengths: int32 [32], replicated, may hold values from 1 to 2049, 32768 in all
- out_weight: bfloat16 [5120, 2560], P('tp'), may hold values from -0.078125 to 0.078125
Outputs:
- mixed: bfloat16 [32768, 2560], P(('ctx', 'tp'))
The draws below stay inside these ranges and needn't reach their ends.
Inputs may be any that keep to these rules, and one draw needn't show every extreme that they name: `doc_lengths`: the lengths sum to 32768; none exceeds 2049, and one equals 2049.
All inputs are finite; a program needn't handle non-finite values.
Results may differ from the reference program's by a relative error of at most 0.018.
Values may be sent and summed in bfloat16 or wider, within the bound.
A program may use at most 64 MiB of HBM per device.

```python
import math
import jax
import jax.numpy as jnp
import numpy as np
from jax import lax

HEADS = 40
KV_HEADS = 8
HEAD_DIM = 128
OUT_COLS = 2560
SPAN = 4
TOK_DEV = 512
TOKENS = 32768
DOCS = 32
MOST = 2049
N_CTX = 64
N_TP = 8


def shared_fields(key):
    base_key = jax.random.fold_in(key, 41)
    keys_split = jax.random.split(base_key, 3)
    kv_width = KV_HEADS * HEAD_DIM
    keys_base = jnp.clip(jax.random.normal(keys_split[0], (TOKENS, kv_width), jnp.float32), -6.0, 6.0)
    values_base = jnp.clip(jax.random.normal(keys_split[1], (TOKENS, kv_width), jnp.float32), -6.0, 6.0)
    query_base = jnp.clip(jax.random.normal(keys_split[2], (TOKENS, HEADS * HEAD_DIM), jnp.float32), -6.0, 6.0)
    return (query_base, keys_base, values_base)


def draw_queries(key, part):
    query_base, keys_base, values_base = shared_fields(key)
    return query_base.astype(jnp.bfloat16)


def draw_keys_values(key, part):
    query_base, keys_base, values_base = shared_fields(key)
    return jnp.stack([keys_base, values_base], axis=0).astype(jnp.bfloat16)


def steps_of(stream_key, extent, pieces, smallest, top_value):
    loudness = 1.0
    for position, parts in pieces:
        heights = jax.random.uniform(jax.random.fold_in(jax.random.fold_in(stream_key, 6), position), (parts,), jnp.float32, smallest / len(pieces), top_value / len(pieces))
        loudness = loudness * jnp.repeat(jnp.exp(heights), extent[position] // parts).reshape((-1,) + (1,) * (len(extent) - 1 - position))
    return loudness


def profile(count, total, most, lean):
    weights = [(1 << 20) // math.isqrt(rank ** lean) + 1 for rank in range(2, count + 1)]
    rest, counts = total - most - (count - 1), [1] * (count - 1)
    while rest > 0:
        candidates = [i for i in range(count - 1) if counts[i] < most]
        whole, remaining = sum([weights[i] for i in candidates]), rest
        for i in candidates:
            more = min(most - counts[i], max(1, remaining * weights[i] // whole), rest)
            counts[i] = counts[i] + more
            rest = rest - more
    return np.array([most] + counts)


def uneven_parts(own_key, number_of, total, most, slope):
    if number_of == 2:
        one = jax.random.randint(own_key, (), max(1, total - most), min(most, total - 1) + 1)
        return jnp.stack([one, total - one])
    lengths = jnp.asarray(profile(number_of, total, most, slope), jnp.int32)
    twos = (number_of - 1) // 2
    giver, receiver = lengths[1:1 + 2 * twos:2], lengths[2:2 + 2 * twos:2]
    slack = jnp.minimum(giver - 1, most - receiver)
    shifted = jax.random.randint(jax.random.fold_in(own_key, 1), (twos,), 0, 1 << 20) % (slack + 1)
    lengths = lengths.at[1:1 + 2 * twos:2].set(giver - shifted).at[2:2 + 2 * twos:2].set(receiver + shifted)
    return lengths[jax.random.permutation(jax.random.fold_in(own_key, 2), number_of)]


def bell_draw(stream_key, dims, deviation, bound, cuts=(), kind=jnp.bfloat16):
    level = steps_of(stream_key, dims, cuts, -0.22, 0.18) if cuts else 1.0
    array = jax.random.normal(stream_key, dims, jnp.float32) * deviation * level
    return jnp.minimum(jnp.maximum(array, -bound), bound).astype(kind)


def setup_inputs(seed: int = 0) -> dict:
    splits = jax.random.split(jax.random.key(seed), 5)
    queries = draw_queries(jax.random.fold_in(splits[4], 71), 0)
    keys_values = draw_keys_values(jax.random.fold_in(splits[4], 71), 0)
    doc_lengths = uneven_parts(splits[2], DOCS, TOKENS, MOST, 2).astype(jnp.int32)
    out_weight = bell_draw(splits[3], (HEADS * HEAD_DIM, OUT_COLS), (HEADS * HEAD_DIM) ** -0.5, 0.078125, ((0, 8),))
    return dict(queries=queries, keys_values=keys_values, doc_lengths=doc_lengths, out_weight=out_weight)


def reference(queries, keys_values, doc_lengths, out_weight):
    group_size = HEADS // KV_HEADS
    score_scale = 1.0 / math.sqrt(HEAD_DIM)
    window = (SPAN + 1) * TOK_DEV
    padding = SPAN * TOK_DEV
    kv_width = KV_HEADS * HEAD_DIM
    doc_ends = jnp.cumsum(doc_lengths).astype(jnp.int32)
    positions = jnp.arange(TOKENS, dtype=jnp.int32)
    doc_ids = lax.optimization_barrier(jnp.sum((positions[:, None] >= doc_ends[None, :]).astype(jnp.int32), axis=1)).astype(jnp.int32)
    pad_rows = jnp.zeros((padding, kv_width), keys_values.dtype)
    keys_pad = jnp.concatenate([pad_rows, keys_values[0]], axis=0)
    values_pad = jnp.concatenate([pad_rows, keys_values[1]], axis=0)
    docs_pad = jnp.concatenate([jnp.full((padding,), -1, jnp.int32), doc_ids], axis=0)

    def one_block(block_idx):
        first_row = (block_idx * TOK_DEV).astype(jnp.int32)
        query_blk = lax.dynamic_slice_in_dim(queries, first_row, TOK_DEV, 0).astype(jnp.float32)
        query_blk = query_blk.reshape(TOK_DEV, KV_HEADS, group_size, HEAD_DIM)
        key_blk = lax.dynamic_slice_in_dim(keys_pad, first_row, window, 0).astype(jnp.float32).reshape(window, KV_HEADS, HEAD_DIM)
        value_blk = lax.dynamic_slice_in_dim(values_pad, first_row, window, 0).astype(jnp.float32).reshape(window, KV_HEADS, HEAD_DIM)
        query_doc = lax.dynamic_slice_in_dim(doc_ids, first_row, TOK_DEV, 0)
        key_doc = lax.dynamic_slice_in_dim(docs_pad, first_row, window, 0)
        query_pos = first_row + jnp.arange(TOK_DEV, dtype=jnp.int32)
        key_pos = first_row - padding + jnp.arange(window, dtype=jnp.int32)
        allowed = (query_doc[:, None] == key_doc[None, :]) & (key_pos[None, :] <= query_pos[:, None])
        scores = jnp.einsum('qkgd,skd->qkgs', query_blk, key_blk, precision=lax.Precision.HIGHEST) * score_scale
        scores = jnp.where(allowed[:, None, None, :], scores, jnp.float32(-1e+30))
        row_max = lax.optimization_barrier(jnp.max(scores, axis=-1, keepdims=True))
        weights = jnp.exp(scores - row_max)
        totals = lax.optimization_barrier(jnp.sum(weights, axis=-1))
        rounded = weights.astype(jnp.bfloat16).astype(jnp.float32)
        summed = jnp.einsum('qkgs,skd->qkgd', rounded, value_blk, precision=lax.Precision.HIGHEST)
        result = summed / totals[..., None]
        return result.reshape(TOK_DEV, HEADS * HEAD_DIM).astype(jnp.bfloat16)
    attended = lax.map(one_block, jnp.arange(N_CTX, dtype=jnp.int32)).reshape(TOKENS, HEADS * HEAD_DIM)
    group_rows = HEADS * HEAD_DIM // N_TP
    mixed_sum = jnp.zeros((TOKENS, OUT_COLS), jnp.float32)
    for tp_group in range(N_TP):
        partial_value = jnp.dot(attended[:, tp_group * group_rows:(tp_group + 1) * group_rows], out_weight[tp_group * group_rows:(tp_group + 1) * group_rows], preferred_element_type=jnp.float32).astype(jnp.bfloat16)
        mixed_sum = mixed_sum + lax.optimization_barrier(partial_value).astype(jnp.float32)
    return mixed_sum.astype(jnp.bfloat16)
```

```python
import math

import jax
import jax.numpy as jnp
from jax import lax
from jax.experimental import pallas as pl
from jax.experimental.pallas import tpu as pltpu
from jax.sharding import PartitionSpec as P

HEAD_DIM = 128
SPAN = 4
TILE = 128
LOW = -(2.0**100)
LOGICAL = pl.DeviceIdType.MESH
FAR = 3


def kernel(
    doc_ref, q_hbm, kv_hbm, w_hbm, out_ref,
    qs, qe, ke, kvb, relay, top, acc, att, att_sib, wbuf, pbuf, step_in, fwd, near, last, mine,
    q_sem, kv_sem, w_sem,
    up_send, up_recv, down_send, down_recv, w_send, w_recv, att_send, att_recv,
    s1_send, s1_recv, near_send, near_recv, last_send, last_recv, mine_send, mine_recv,
):
    n_ctx = lax.axis_size("ctx")
    n_rows = kvb.shape[2]
    n_tiles = n_rows // TILE
    heads = qs.shape[1] // TILE
    docs = doc_ref.shape[0]
    half_cols = pbuf.shape[3]
    me = lax.axis_index("ctx")
    tp = lax.axis_index("tp")
    x = tp // 2
    core = tp % 2
    x1 = x + 1 - 2 * (x % 2)
    x2 = (x + 2) % 4
    x3 = 3 - x
    up = (me + 1) % n_ctx
    down = (me + n_ctx - 1) % n_ctx
    jump = (me + 5) % n_ctx
    back = (me + n_ctx - 5) % n_ctx
    sib = x * 2 + 1 - core

    barrier = pltpu.get_barrier_semaphore()
    friends = [(up, tp), (down, tp), (jump, tp), (back, tp), (me, sib)]
    friends += [(me, x1 * 2 + k) for k in range(2)] + [(me, x3 * 2 + k) for k in range(2)]
    for friend in friends:
        pl.semaphore_signal(barrier, inc=1, device_id=friend, device_id_type=LOGICAL)

    q_copies = [
        pltpu.make_async_copy(
            q_hbm.at[:, :, pl.ds(h * HEAD_DIM, HEAD_DIM)],
            qs.at[:, pl.ds(h * TILE, TILE), :],
            q_sem.at[h],
        )
        for h in range(heads)
    ]
    kv_copy = pltpu.make_async_copy(kv_hbm, kvb.at[0], kv_sem)
    my_cols = pl.ds(pl.multiple_of(core * 2 * half_cols, 128), 2 * half_cols)
    sib_cols = pl.ds(pl.multiple_of((1 - core) * 2 * half_cols, 128), 2 * half_cols)
    w_copy = pltpu.make_async_copy(w_hbm.at[:, my_cols], wbuf.at[0], w_sem)
    kv_copy.start()
    for c in q_copies:
        c.start()

    def remote(src, dst, send, recv, to):
        return pltpu.make_async_remote_copy(
            src_ref=src, dst_ref=dst, send_sem=send, recv_sem=recv, device_id=to, device_id_type=LOGICAL
        )

    def piece(ref, c):
        return ref.at[:, pl.ds(c * TILE, TILE), :]

    def up_copy(j, c):
        src = piece(kv_hbm if j == 1 else kvb.at[j - 1], c)
        return remote(src, piece(kvb.at[j], c), up_send.at[j - 1, c], up_recv.at[j - 1, c], (up, tp))

    def down_copy(j):
        if j == 5:
            return remote(piece(kv_hbm, FAR), relay, down_send.at[4], down_recv.at[4], (jump, tp))
        src = relay if j == 4 else piece(kvb.at[j + 1], FAR)
        return remote(src, piece(kvb.at[j], FAR), down_send.at[j - 1], down_recv.at[j - 1], (down, tp))

    w_remote = remote(w_hbm.at[:, sib_cols], wbuf.at[1], w_send, w_recv, (me, sib))

    lane = lax.broadcasted_iota(jnp.int32, (1, 128), 1)
    low_end = jnp.zeros((1, 128), jnp.int32)
    high_end = jnp.zeros((1, 128), jnp.int32)
    end = jnp.int32(0)
    for d in range(docs):
        low_end = jnp.where(lane == d, end, low_end)
        end = end + doc_ref[d]
        high_end = jnp.where(lane == d, end, high_end)
    row = lax.broadcasted_iota(jnp.int32, (n_rows, 128), 0)

    def inside(offset):
        pos = row + (me - offset) * n_rows
        return (pos >= low_end) & (pos < high_end)

    qe[...] = jnp.where(inside(0), 1.0, 0.0).astype(jnp.bfloat16).reshape(qe.shape)
    ke[0] = jnp.where(inside(0), 0.0, LOW).astype(jnp.bfloat16)

    pl.semaphore_wait(barrier, len(friends))
    ups, downs = {}, {}
    order = list(range(FAR))[::-1]
    for c in order:
        ups[1, c] = up_copy(1, c)
        ups[1, c].start()
    downs[5] = down_copy(5)
    downs[5].start()
    w_remote.start()
    w_copy.start()

    for j in range(1, SPAN + 1):
        ke[j] = jnp.where(inside(j), 0.0, LOW).astype(jnp.bfloat16)

    def got_up(j, c):
        ups[j, c].wait_recv()
        if j < SPAN:
            ups[j + 1, c] = up_copy(j + 1, c)
            ups[j + 1, c].start()

    def got_down(j):
        downs[j].wait_recv()
        if j > 1:
            downs[j - 1] = down_copy(j - 1)
            downs[j - 1].start()

    scale = math.log2(math.e) / math.sqrt(HEAD_DIM)

    def keys_of(spans):
        k = jnp.concatenate([kvb[j, 0, r : r + n, :] for j, r, n in spans], axis=0)
        e = jnp.concatenate([ke[j, r : r + n, :] for j, r, n in spans], axis=0)
        return jnp.concatenate([k, e], axis=1)

    def values_of(spans):
        v = jnp.concatenate([kvb[j, 1, r : r + n, :] for j, r, n in spans], axis=0)
        return jnp.concatenate([v, jnp.ones_like(v)], axis=1)

    def scores(item):
        t, spans, first = item
        q = jnp.concatenate([qs[t], jnp.concatenate([qe[t]] * heads, axis=0)], axis=1)
        s = lax.dot_general(q, keys_of(spans), (((1,), (1,)), ((), ())), preferred_element_type=jnp.float32)
        if first:
            n = s.shape[1]
            shape = (TILE * heads, TILE)
            key = lax.broadcasted_iota(jnp.int32, shape, 1)
            query = lax.broadcasted_iota(jnp.int32, (heads, TILE, TILE), 1).reshape(shape)
            own = jnp.where(key <= query, s[:, n - TILE :], LOW)
            s = own if n == TILE else jnp.concatenate([s[:, : n - TILE], own], axis=1)
        return s

    def soften(item, s):
        t, _, first = item
        copies = s.shape[1] // 128
        most = jnp.broadcast_to(jnp.max(s, axis=1, keepdims=True), (s.shape[0], 128))
        if first:
            factor = None
        else:
            before = top[t]
            most = jnp.maximum(before, most)
            factor = jnp.exp2((before - most) * scale)
        weights = jnp.exp2((s - jnp.concatenate([most] * copies, axis=1)) * scale).astype(jnp.bfloat16)
        top[t] = most
        return weights, factor

    def gather(item, weights, factor):
        t, spans, first = item
        part = jnp.dot(weights, values_of(spans), preferred_element_type=jnp.float32)
        if first:
            acc[t] = part
        else:
            acc[t] = acc[t] * jnp.concatenate([factor, factor], axis=1) + part

    def attend(items):
        held = scores(items[0])
        pending = None
        for i, item in enumerate(items):
            following = scores(items[i + 1]) if i + 1 < len(items) else None
            now = soften(item, held)
            if pending is not None:
                gather(*pending)
            pending = (item, *now)
            held = following
        gather(*pending)

    kv_copy.wait()
    for c in q_copies:
        c.wait()
    attend([(t, [(0, 0, (t + 1) * TILE)], True) for t in range(n_tiles)])

    def block(n):
        return [(n, 0, FAR * TILE), (5 - n, FAR * TILE, TILE)]

    got_up(1, 2)
    got_up(1, 1)
    got_up(1, 0)
    got_down(5)
    got_up(2, 2)
    got_down(4)
    attend([(t, block(1), False) for t in (0, 1)])
    got_up(2, 1)
    attend([(t, block(1), False) for t in (2, 3)])
    got_up(2, 0)
    got_up(3, 2)
    got_down(3)
    attend([(t, block(2), False) for t in (0, 1)])
    got_up(3, 1)
    attend([(t, block(2), False) for t in (2, 3)])
    got_up(3, 0)
    got_down(2)
    attend([(t, block(3), False) for t in (0, 1)])
    got_up(4, 2)
    attend([(t, block(3), False) for t in (2, 3)])
    got_up(4, 1)
    got_down(1)
    lasts = []
    for t in (3, 2, 1, 0):
        spans = [(1, FAR * TILE, TILE)]
        first_row = max(t, 1) * TILE
        if first_row < FAR * TILE:
            spans = [(4, first_row, FAR * TILE - first_row)] + spans
        lasts.append((t, spans, False))
    attend(lasts)
    got_up(4, 0)
    attend([(0, [(4, 0, TILE)], False)])

    att_copies = {}
    for place, t in enumerate((x2, x1, x3, x)):
        a = acc[t]
        whole = (a[:, :HEAD_DIM] / a[:, HEAD_DIM:]).astype(jnp.bfloat16)
        for h in range(heads):
            att[place, :, h * HEAD_DIM : (h + 1) * HEAD_DIM] = whole[h * TILE : (h + 1) * TILE, :]
        att_copies[place] = remote(
            att.at[place], att_sib.at[place], att_send.at[place], att_recv.at[place], (me, sib)
        )
        att_copies[place].start()

    w_copy.wait()
    w_remote.wait()
    sends = []

    def project(place):
        att_copies[place].wait()
        for side in range(2):
            cols = slice(side * half_cols, (side + 1) * half_cols)
            part = jnp.dot(att[place], wbuf[0, :, cols], preferred_element_type=jnp.float32)
            part = part + jnp.dot(att_sib[place], wbuf[1, :, cols], preferred_element_type=jnp.float32)
            pbuf[place, side] = part.astype(jnp.bfloat16)

    def send(copy):
        copy.start()
        sends.append(copy)
        return copy

    rows_out = TILE // 2
    partner = (x1, x3)

    def to_cores(src, dst, send_sem, recv_sem, side, chip):
        for k in range(2):
            send(
                remote(
                    src.at[pl.ds(k * rows_out, rows_out), :],
                    dst.at[core, side],
                    send_sem.at[side, k],
                    recv_sem.at[core, side],
                    (me, chip * 2 + k),
                )
            )

    project(0)
    hops = [
        send(remote(pbuf.at[0, side], step_in.at[side], s1_send.at[side], s1_recv.at[side], (me, partner[side] * 2 + core)))
        for side in range(2)
    ]
    project(1)
    to_cores(pbuf.at[1, 0], near, near_send, near_recv, 0, x1)
    project(2)
    to_cores(pbuf.at[2, 1], near, near_send, near_recv, 1, x3)
    project(3)
    other = pl.multiple_of((1 - core) * rows_out, rows_out)
    own = pl.multiple_of(core * rows_out, rows_out)
    mine_copy = send(
        remote(pbuf.at[3, :, pl.ds(other, rows_out), :], mine, mine_send, mine_recv, (me, sib))
    )
    for side in range(2):
        hops[side].wait_recv()
        held = pbuf[2 - side, side].astype(jnp.float32) + step_in[side].astype(jnp.float32)
        fwd[side] = held.astype(jnp.bfloat16)
        to_cores(fwd.at[side], last, last_send, last_recv, side, partner[1 - side])

    def arrived(buf, sems_s, sems_r, k, side):
        remote(buf.at[k, side], buf.at[k, side], sems_s.at[side, 0], sems_r.at[k, side], (me, sib)).wait_recv()

    mine_copy.wait_recv()
    for k in range(2):
        for side in range(2):
            arrived(near, near_send, near_recv, k, side)
    for side in range(2):
        for k in range(2):
            arrived(last, last_send, last_recv, k, side)
            here = pbuf[3, side, pl.ds(own, rows_out), :].astype(jnp.float32)
            there = mine[side].astype(jnp.float32)
            base = jnp.where(core == k, here, there)
            total = base + near[k, side].astype(jnp.float32) + last[k, side].astype(jnp.float32)
            col = (2 * k + side) * half_cols
            out_ref[:, col : col + half_cols] = total.astype(jnp.bfloat16)

    for copy in sends:
        copy.wait_send()
    for copy in ups.values():
        copy.wait_send()
    for copy in downs.values():
        copy.wait_send()


def on_device(queries, keys_values, doc_lengths, out_weight):
    rows, width = queries.shape
    cols = out_weight.shape[1]
    heads = width // HEAD_DIM
    tiles = rows // TILE
    half = cols // 4
    n_tp = lax.axis_size("tp")
    bf, f32 = jnp.bfloat16, jnp.float32
    dma = pltpu.SemaphoreType.DMA
    hbm = pl.BlockSpec(memory_space=pl.ANY)
    return pl.pallas_call(
        kernel,
        out_shape=jax.ShapeDtypeStruct((rows // n_tp, cols), bf),
        in_specs=[pl.BlockSpec(memory_space=pltpu.SMEM), hbm, hbm, hbm],
        out_specs=pl.BlockSpec(memory_space=pltpu.VMEM),
        scratch_shapes=[
            pltpu.VMEM((tiles, heads * TILE, HEAD_DIM), bf),
            pltpu.VMEM((tiles, TILE, 128), bf),
            pltpu.VMEM((SPAN + 1, rows, 128), bf),
            pltpu.VMEM((SPAN + 1, 2, rows, HEAD_DIM), bf),
            pltpu.VMEM((2, TILE, HEAD_DIM), bf),
            pltpu.VMEM((tiles, heads * TILE, 128), f32),
            pltpu.VMEM((tiles, heads * TILE, 2 * HEAD_DIM), f32),
            pltpu.VMEM((tiles, TILE, width), bf),
            pltpu.VMEM((tiles, TILE, width), bf),
            pltpu.VMEM((2, width, cols // 2), bf),
            pltpu.VMEM((tiles, 2, TILE, half), bf),
            pltpu.VMEM((2, TILE, half), bf),
            pltpu.VMEM((2, TILE, half), bf),
            pltpu.VMEM((2, 2, TILE // 2, half), bf),
            pltpu.VMEM((2, 2, TILE // 2, half), bf),
            pltpu.VMEM((2, TILE // 2, half), bf),
            dma((heads,)), dma, dma,
            dma((SPAN, FAR)), dma((SPAN, FAR)), dma((5,)), dma((5,)), dma, dma, dma((4,)), dma((4,)),
            dma((2,)), dma((2,)), dma((2, 2)), dma((2, 2)), dma((2, 2)), dma((2, 2)), dma, dma,
        ],
        compiler_params=pltpu.CompilerParams(
            collective_id=0, has_side_effects=True, vmem_limit_bytes=56 << 20
        ),
        cost_estimate=pl.CostEstimate(flops=8_000_000_000, bytes_accessed=8_000_000, transcendentals=6_000_000),
        name="attend_project",
    )(doc_lengths, queries.reshape(tiles, TILE, width), keys_values, out_weight)


def solution(mesh):
    placed = (P("ctx", "tp"), P(None, "ctx", "tp"), P(), P("tp", None))
    return jax.shard_map(
        on_device, mesh=mesh, in_specs=placed, out_specs=P(("ctx", "tp"), None), check_vma=False
    )
```

```python
import math

import jax
import jax.numpy as jnp
from jax import lax
from jax.experimental import pallas as pl
from jax.experimental.pallas import tpu as pltpu
from jax.sharding import PartitionSpec as P

HEAD_DIM = 128
SPAN = 4
TILE = 128
LOW = -(2.0**100)
LOGICAL = pl.DeviceIdType.MESH
FAR = 3
PART = TILE // 2


def kernel(
    doc_ref, q_hbm, kv_hbm, w_hbm, out_ref,
    qs, qe, ke, kvb, relay, top, acc, att, att_sib, wbuf, pbuf, step_in, fwd, near, last, mine,
    q_sem, kv_sem, w_sem,
    up_send, up_recv, jump_send, jump_recv, down_send, down_recv, end_send, w_send, w_recv, att_send, att_recv,
    s1_send, s1_recv, near_send, near_recv, last_send, last_recv, mine_send, mine_recv, ready,
):
    n_ctx = lax.axis_size("ctx")
    n_rows = kvb.shape[2]
    n_tiles = n_rows // TILE
    heads = qs.shape[1] // TILE
    docs = doc_ref.shape[0]
    half_cols = pbuf.shape[3]
    me = lax.axis_index("ctx")
    tp = lax.axis_index("tp")
    x = tp // 2
    core = tp % 2
    x1 = x + 1 - 2 * (x % 2)
    x2 = (x + 2) % 4
    x3 = 3 - x
    end_ctx = n_ctx - 1
    sib = x * 2 + 1 - core

    def ahead(by):
        return jnp.minimum(me + by, end_ctx), tp

    def behind(by):
        return jnp.maximum(me - by, 0), tp

    barrier = pltpu.get_barrier_semaphore()

    def tell(semaphore, who):
        pl.semaphore_signal(semaphore, inc=1, device_id=who, device_id_type=LOGICAL)

    def if_ahead(by):
        return pl.when(me + by <= end_ctx)

    def if_behind(by):
        return pl.when(me >= by)

    n_friends = 5
    for by in range(1, SPAN + 2):

        @if_ahead(by)
        def _(by=by):
            tell(barrier, ahead(by))

        n_friends = n_friends + jnp.where(me >= by, 1, 0)

    @if_behind(1)
    def _():
        tell(barrier, behind(1))

    n_friends = n_friends + jnp.where(me < end_ctx, 1, 0)
    tell(barrier, (me, sib))
    for chip in (x1, x3):
        for k in range(2):
            tell(barrier, (me, chip * 2 + k))

    q_copies = [
        pltpu.make_async_copy(
            q_hbm.at[:, :, pl.ds(h * HEAD_DIM, HEAD_DIM)],
            qs.at[:, pl.ds(h * TILE, TILE), :],
            q_sem.at[h],
        )
        for h in range(heads)
    ]
    kv_copy = pltpu.make_async_copy(kv_hbm, kvb.at[0], kv_sem)
    my_cols = pl.ds(pl.multiple_of(core * 2 * half_cols, 128), 2 * half_cols)
    sib_cols = pl.ds(pl.multiple_of((1 - core) * 2 * half_cols, 128), 2 * half_cols)
    w_copy = pltpu.make_async_copy(w_hbm.at[:, my_cols], wbuf.at[0], w_sem)
    kv_copy.start()
    for c in q_copies:
        c.start()

    def remote(src, dst, send, recv, to):
        return pltpu.make_async_remote_copy(
            src_ref=src, dst_ref=dst, send_sem=send, recv_sem=recv, device_id=to, device_id_type=LOGICAL
        )

    def piece(ref, c):
        return ref.at[:, pl.ds(c * TILE, TILE), :]

    def up_copy(j, c):
        src = piece(kv_hbm if j == 1 else kvb.at[j - 1], c)
        return remote(src, piece(kvb.at[j], c), up_send.at[j - 1, c], up_recv.at[j - 1, c], ahead(1))

    def part(ref, e):
        return ref.at[:, pl.ds(FAR * TILE + e * PART, PART), :]

    def jump_copy(e):
        return remote(part(kv_hbm, e), relay.at[e], jump_send.at[e], jump_recv.at[e], ahead(SPAN + 1))

    def down_copy(j, e):
        return remote(
            relay.at[e], part(kvb.at[j], e), down_send.at[j - 2, e], down_recv.at[j - 2, e], behind(SPAN + 1 - j)
        )

    def end_copy(j, e):
        return remote(
            part(kv_hbm, e), part(kvb.at[j], e), end_send.at[j - 2, e], down_recv.at[j - 2, e], ahead(j)
        )

    w_remote = remote(w_hbm.at[:, sib_cols], wbuf.at[1], w_send, w_recv, (me, sib))

    lane = lax.broadcasted_iota(jnp.int32, (1, 128), 1)
    low_end = jnp.zeros((1, 128), jnp.int32)
    high_end = jnp.zeros((1, 128), jnp.int32)
    end = jnp.int32(0)
    for d in range(docs):
        low_end = jnp.where(lane == d, end, low_end)
        end = end + doc_ref[d]
        high_end = jnp.where(lane == d, end, high_end)
    row = lax.broadcasted_iota(jnp.int32, (n_rows, 128), 0)

    def inside(offset):
        pos = row + (me - offset) * n_rows
        return (pos >= low_end) & (pos < high_end)

    qe[...] = jnp.where(inside(0), 1.0, 0.0).astype(jnp.bfloat16).reshape(qe.shape)
    ke[0] = jnp.where(inside(0), 0.0, LOW).astype(jnp.bfloat16)

    for j in range(1, SPAN + 1):

        @pl.when(me < j)
        def _(j=j):
            kvb[j] = jnp.zeros(kvb.shape[1:], kvb.dtype)

    pl.semaphore_wait(barrier, n_friends)

    def start_own(c):
        @if_ahead(1)
        def _():
            up_copy(1, c).start()

    start_own(FAR)

    @if_behind(SPAN + 1)
    def _():
        tell(ready, behind(SPAN + 1))

    for j in range(2, SPAN + 1):

        @pl.when((me >= j) & (me - j + SPAN + 1 > end_ctx))
        def _(j=j):
            tell(ready, behind(j))

    w_copy.start()

    def start_jump(e):
        @if_ahead(SPAN + 1)
        def _():
            if e == 0:
                pl.semaphore_wait(ready, 1)
            jump_copy(e).start()

        @pl.when(me + SPAN + 1 > end_ctx)
        def _():
            if e == 0:

                @if_ahead(2)
                def _():
                    pl.semaphore_wait(ready, jnp.minimum(end_ctx - me, SPAN) - 1)

            for j in range(2, SPAN + 1):

                @if_ahead(j)
                def _(j=j):
                    end_copy(j, e).start()

    for j in range(1, SPAN + 1):
        ke[j] = jnp.where(inside(j), 0.0, LOW).astype(jnp.bfloat16)

    def got_up(j, c):
        @if_behind(j)
        def _():
            up_copy(j, c).wait_recv()
            if j < SPAN and c < FAR:

                @if_ahead(1)
                def _():
                    up_copy(j + 1, c).start()

    def got_jump(e):
        @if_behind(SPAN + 1)
        def _():
            jump_copy(e).wait_recv()
            for j in (2, 3, 4):
                down_copy(j, e).start()

    def got_down(j, e):
        @if_behind(j)
        def _():
            down_copy(j, e).wait_recv()

    scale = math.log2(math.e) / math.sqrt(HEAD_DIM)

    def keys_of(spans):
        k = jnp.concatenate([kvb[j, 0, r : r + n, :] for j, r, n in spans], axis=0)
        e = jnp.concatenate([ke[j, r : r + n, :] for j, r, n in spans], axis=0)
        return jnp.concatenate([k, e], axis=1)

    def values_of(spans):
        v = jnp.concatenate([kvb[j, 1, r : r + n, :] for j, r, n in spans], axis=0)
        return jnp.concatenate([v, jnp.ones_like(v)], axis=1)

    def scores(item):
        t, spans, first = item
        q = jnp.concatenate([qs[t], jnp.concatenate([qe[t]] * heads, axis=0)], axis=1)
        s = lax.dot_general(q, keys_of(spans), (((1,), (1,)), ((), ())), preferred_element_type=jnp.float32)
        if first:
            n = s.shape[1]
            shape = (TILE * heads, TILE)
            key = lax.broadcasted_iota(jnp.int32, shape, 1)
            query = lax.broadcasted_iota(jnp.int32, (heads, TILE, TILE), 1).reshape(shape)
            own = jnp.where(key <= query, s[:, n - TILE :], LOW)
            s = own if n == TILE else jnp.concatenate([s[:, : n - TILE], own], axis=1)
        return s

    def soften(item, s):
        t, _, first = item
        copies = s.shape[1] // 128
        most = jnp.broadcast_to(jnp.max(s, axis=1, keepdims=True), (s.shape[0], 128))
        if first:
            factor = None
        else:
            before = top[t]
            most = jnp.maximum(before, most)
            factor = jnp.exp2((before - most) * scale)
        weights = jnp.exp2((s - jnp.concatenate([most] * copies, axis=1)) * scale).astype(jnp.bfloat16)
        top[t] = most
        return weights, factor

    def gather(item, weights, factor):
        t, spans, first = item
        part = jnp.dot(weights, values_of(spans), preferred_element_type=jnp.float32)
        if first:
            acc[t] = part
        else:
            acc[t] = acc[t] * jnp.concatenate([factor, factor], axis=1) + part

    def attend(items):
        held = scores(items[0])
        pending = None
        for i, item in enumerate(items):
            following = scores(items[i + 1]) if i + 1 < len(items) else None
            now = soften(item, held)
            if pending is not None:
                gather(*pending)
            pending = (item, *now)
            held = following
        gather(*pending)

    kv_copy.wait()
    for c in q_copies:
        c.wait()
    first = [(t, [(0, 0, (t + 1) * TILE)], True) for t in range(n_tiles)]
    attend(first[:2])
    start_own(2)
    attend(first[2:3])
    start_own(1)
    attend(first[3:])
    start_own(0)
    w_remote.start()

    def whole(n, rows):
        return [(t, [(n, 0, rows)], False) for t in range(n_tiles)]

    got_up(1, 3)
    got_up(1, 2)
    start_jump(0)
    got_up(1, 1)
    start_jump(1)
    got_up(1, 0)
    attend(whole(1, n_rows)[:2])
    got_up(2, 2)
    attend(whole(1, n_rows)[2:])
    got_up(2, 1)
    got_jump(0)
    got_up(2, 0)
    got_jump(1)
    attend(whole(2, FAR * TILE)[:2])
    got_up(3, 2)
    attend(whole(2, FAR * TILE)[2:])
    got_up(3, 1)
    got_up(3, 0)
    attend(whole(3, FAR * TILE)[:2])
    got_up(4, 2)
    attend(whole(3, FAR * TILE)[2:])
    for e in range(2):
        for j in (4, 3, 2):
            got_down(j, e)
    attend([(t, [(j, FAR * TILE, TILE) for j in (4, 3, 2)], False) for t in range(n_tiles)])
    got_up(4, 1)

    def finish(t):
        a = acc[t]
        done = (a[:, :HEAD_DIM] / a[:, HEAD_DIM:]).astype(jnp.bfloat16)
        for h in range(heads):
            att[t, :, h * HEAD_DIM : (h + 1) * HEAD_DIM] = done[h * TILE : (h + 1) * TILE, :]
        att_copy(t).start()

    def att_copy(t):
        return remote(att.at[t], att_sib.at[t], att_send.at[t], att_recv.at[t], (me, sib))

    attend([(t, [(SPAN, max(t, 1) * TILE, (FAR - max(t, 1)) * TILE)], False) for t in (2, 1, 0)])
    for t in (3, 2, 1):
        finish(t)
    got_up(4, 0)
    attend([(0, [(SPAN, 0, TILE)], False)])
    finish(0)

    w_copy.wait()
    w_remote.wait()
    sends = []

    def project(place):
        t = (x2, x1, x3, x)[place]
        att_copy(t).wait_recv()
        for side in range(2):
            cols = slice(side * half_cols, (side + 1) * half_cols)
            total = jnp.dot(att[t], wbuf[0, :, cols], preferred_element_type=jnp.float32)
            total = total + jnp.dot(att_sib[t], wbuf[1, :, cols], preferred_element_type=jnp.float32)
            pbuf[place, side] = total.astype(jnp.bfloat16)

    def send(copy):
        copy.start()
        sends.append(copy)
        return copy

    rows_out = TILE // 2
    partner = (x1, x3)

    def to_cores(src, dst, send_sem, recv_sem, side, chip):
        for k in range(2):
            send(
                remote(
                    src.at[pl.ds(k * rows_out, rows_out), :],
                    dst.at[core, side],
                    send_sem.at[side, k],
                    recv_sem.at[core, side],
                    (me, chip * 2 + k),
                )
            )

    project(0)
    hops = [
        remote(pbuf.at[0, side], step_in.at[side], s1_send.at[side], s1_recv.at[side], (me, partner[side] * 2 + core))
        for side in range(2)
    ]
    for hop in hops:
        hop.start()
    for place in (1, 2, 3):
        project(place)
    to_cores(pbuf.at[1, 0], near, near_send, near_recv, 0, x1)
    to_cores(pbuf.at[2, 1], near, near_send, near_recv, 1, x3)
    other = pl.multiple_of((1 - core) * rows_out, rows_out)
    own = pl.multiple_of(core * rows_out, rows_out)
    mine_copy = send(
        remote(pbuf.at[3, :, pl.ds(other, rows_out), :], mine, mine_send, mine_recv, (me, sib))
    )
    for side in range(2):
        hops[side].wait_recv()
        sends.append(hops[side])
        held = pbuf[2 - side, side].astype(jnp.float32) + step_in[side].astype(jnp.float32)
        fwd[side] = held.astype(jnp.bfloat16)
        to_cores(fwd.at[side], last, last_send, last_recv, side, partner[1 - side])

    def arrived(buf, sems_s, sems_r, k, side):
        remote(buf.at[k, side], buf.at[k, side], sems_s.at[side, 0], sems_r.at[k, side], (me, sib)).wait_recv()

    mine_copy.wait_recv()
    for k in range(2):
        for side in range(2):
            arrived(near, near_send, near_recv, k, side)
    for side in range(2):
        for k in range(2):
            arrived(last, last_send, last_recv, k, side)
            here = pbuf[3, side, pl.ds(own, rows_out), :].astype(jnp.float32)
            there = mine[side].astype(jnp.float32)
            base = jnp.where(core == k, here, there)
            total = base + near[k, side].astype(jnp.float32) + last[k, side].astype(jnp.float32)
            col = (2 * k + side) * half_cols
            out_ref[:, col : col + half_cols] = total.astype(jnp.bfloat16)

    for copy in sends:
        copy.wait_send()
    for t in range(n_tiles):
        att_copy(t).wait_send()

    @if_ahead(1)
    def _():
        for c in range(FAR + 1):
            up_copy(1, c).wait_send()
        for j in range(2, SPAN + 1):

            @if_behind(j - 1)
            def _(j=j):
                for c in range(FAR):
                    up_copy(j, c).wait_send()

    @if_ahead(SPAN + 1)
    def _():
        for e in range(2):
            jump_copy(e).wait_send()

    @if_behind(SPAN + 1)
    def _():
        for e in range(2):
            for j in (2, 3, 4):
                down_copy(j, e).wait_send()

    @pl.when(me + SPAN + 1 > end_ctx)
    def _():
        for j in range(2, SPAN + 1):

            @if_ahead(j)
            def _(j=j):
                for e in range(2):
                    end_copy(j, e).wait_send()


def on_device(queries, keys_values, doc_lengths, out_weight):
    rows, width = queries.shape
    cols = out_weight.shape[1]
    heads = width // HEAD_DIM
    tiles = rows // TILE
    half = cols // 4
    n_tp = lax.axis_size("tp")
    bf, f32 = jnp.bfloat16, jnp.float32
    dma = pltpu.SemaphoreType.DMA
    hbm = pl.BlockSpec(memory_space=pl.ANY)
    return pl.pallas_call(
        kernel,
        out_shape=jax.ShapeDtypeStruct((rows // n_tp, cols), bf),
        in_specs=[pl.BlockSpec(memory_space=pltpu.SMEM), hbm, hbm, hbm],
        out_specs=pl.BlockSpec(memory_space=pltpu.VMEM),
        scratch_shapes=[
            pltpu.VMEM((tiles, heads * TILE, HEAD_DIM), bf),
            pltpu.VMEM((tiles, TILE, 128), bf),
            pltpu.VMEM((SPAN + 1, rows, 128), bf),
            pltpu.VMEM((SPAN + 1, 2, rows, HEAD_DIM), bf),
            pltpu.VMEM((2, 2, PART, HEAD_DIM), bf),
            pltpu.VMEM((tiles, heads * TILE, 128), f32),
            pltpu.VMEM((tiles, heads * TILE, 2 * HEAD_DIM), f32),
            pltpu.VMEM((tiles, TILE, width), bf),
            pltpu.VMEM((tiles, TILE, width), bf),
            pltpu.VMEM((2, width, cols // 2), bf),
            pltpu.VMEM((tiles, 2, TILE, half), bf),
            pltpu.VMEM((2, TILE, half), bf),
            pltpu.VMEM((2, TILE, half), bf),
            pltpu.VMEM((2, 2, TILE // 2, half), bf),
            pltpu.VMEM((2, 2, TILE // 2, half), bf),
            pltpu.VMEM((2, TILE // 2, half), bf),
            dma((heads,)), dma, dma,
            dma((SPAN, FAR + 1)), dma((SPAN, FAR + 1)), dma((2,)), dma((2,)), dma((SPAN - 1, 2)), dma((SPAN - 1, 2)), dma((SPAN - 1, 2)), dma, dma, dma((4,)), dma((4,)),
            dma((2,)), dma((2,)), dma((2, 2)), dma((2, 2)), dma((2, 2)), dma((2, 2)), dma, dma,
            pltpu.SemaphoreType.REGULAR,
        ],
        compiler_params=pltpu.CompilerParams(
            collective_id=0, has_side_effects=True, vmem_limit_bytes=56 << 20
        ),
        cost_estimate=pl.CostEstimate(flops=8_000_000_000, bytes_accessed=8_000_000, transcendentals=6_000_000),
        name="attend_project",
    )(doc_lengths, queries.reshape(tiles, TILE, width), keys_values, out_weight)


def solution(mesh):
    placed = (P("ctx", "tp"), P(None, "ctx", "tp"), P(), P("tp", None))
    return jax.shard_map(
        on_device, mesh=mesh, in_specs=placed, out_specs=P(("ctx", "tp"), None), check_vma=False
    )
```

```python
import math

import jax
import jax.numpy as jnp
from jax import lax
from jax.experimental import pallas as pl
from jax.experimental.pallas import tpu as pltpu
from jax.sharding import PartitionSpec as P

HEAD_DIM = 128
SPAN = 4
TILE = 128
LOW = -(2.0**100)
LOGICAL = pl.DeviceIdType.MESH
FAR = 3
PART = TILE // 2


def kernel(
    doc_hbm, q_hbm, kv_hbm, w_hbm, sum_hbm, last_hbm,
    qs, qe, ke, kvb, relay, top, acc, att, att_sib, wbuf, pbuf, step_in, fwd, near, sums, mine, doc_ref,
    doc_sem, q_sem, kv_sem, w_sem, sum_sem,
    up_send, up_recv, jump_send, jump_recv, down_send, down_recv, end_send, w_send, w_recv, att_send, att_recv,
    s1_send, s1_recv, near_send, near_recv, last_send, last_recv, mine_send, mine_recv, ready,
):
    n_ctx = lax.axis_size("ctx")
    n_rows = kvb.shape[2]
    n_tiles = n_rows // TILE
    heads = qs.shape[1] // TILE
    docs = doc_ref.shape[0]
    half_cols = pbuf.shape[3]
    me = lax.axis_index("ctx")
    tp = lax.axis_index("tp")
    x = tp // 2
    core = tp % 2
    x1 = x + 1 - 2 * (x % 2)
    x2 = (x + 2) % 4
    x3 = 3 - x
    end_ctx = n_ctx - 1
    sib = x * 2 + 1 - core

    def ahead(by):
        return jnp.minimum(me + by, end_ctx), tp

    def behind(by):
        return jnp.maximum(me - by, 0), tp

    doc_copy = pltpu.make_async_copy(doc_hbm, doc_ref, doc_sem)
    doc_copy.start()
    barrier = pltpu.get_barrier_semaphore()

    def tell(semaphore, who):
        pl.semaphore_signal(semaphore, inc=1, device_id=who, device_id_type=LOGICAL)

    def if_ahead(by):
        return pl.when(me + by <= end_ctx)

    def if_behind(by):
        return pl.when(me >= by)

    n_friends = 5
    for by in range(1, SPAN + 2):

        @if_ahead(by)
        def _(by=by):
            tell(barrier, ahead(by))

        n_friends = n_friends + jnp.where(me >= by, 1, 0)

    @if_behind(1)
    def _():
        tell(barrier, behind(1))

    n_friends = n_friends + jnp.where(me < end_ctx, 1, 0)
    tell(barrier, (me, sib))
    for chip in (x1, x3):
        for k in range(2):
            tell(barrier, (me, chip * 2 + k))

    q_copies = [
        pltpu.make_async_copy(
            q_hbm.at[:, :, pl.ds(h * HEAD_DIM, HEAD_DIM)],
            qs.at[:, pl.ds(h * TILE, TILE), :],
            q_sem.at[h],
        )
        for h in range(heads)
    ]
    kv_copy = pltpu.make_async_copy(kv_hbm, kvb.at[0], kv_sem)
    my_cols = pl.ds(pl.multiple_of(core * 2 * half_cols, 128), 2 * half_cols)
    sib_cols = pl.ds(pl.multiple_of((1 - core) * 2 * half_cols, 128), 2 * half_cols)
    w_copy = pltpu.make_async_copy(w_hbm.at[:, my_cols], wbuf.at[0], w_sem)
    kv_copy.start()
    for c in q_copies:
        c.start()

    def remote(src, dst, send, recv, to):
        return pltpu.make_async_remote_copy(
            src_ref=src, dst_ref=dst, send_sem=send, recv_sem=recv, device_id=to, device_id_type=LOGICAL
        )

    def piece(ref, c):
        return ref.at[:, pl.ds(c * TILE, TILE), :]

    def up_copy(j, c):
        src = piece(kv_hbm if j == 1 else kvb.at[j - 1], c)
        return remote(src, piece(kvb.at[j], c), up_send.at[j - 1, c], up_recv.at[j - 1, c], ahead(1))

    def part(ref, e):
        return ref.at[:, pl.ds(FAR * TILE + e * PART, PART), :]

    def jump_copy(e):
        return remote(part(kv_hbm, e), relay.at[e], jump_send.at[e], jump_recv.at[e], ahead(SPAN + 1))

    def down_copy(j, e):
        return remote(
            relay.at[e], part(kvb.at[j], e), down_send.at[j - 2, e], down_recv.at[j - 2, e], behind(SPAN + 1 - j)
        )

    def end_copy(j, e):
        return remote(
            part(kv_hbm, e), part(kvb.at[j], e), end_send.at[j - 2, e], down_recv.at[j - 2, e], ahead(j)
        )

    w_remote = remote(w_hbm.at[:, sib_cols], wbuf.at[1], w_send, w_recv, (me, sib))

    doc_copy.wait()
    lane = lax.broadcasted_iota(jnp.int32, (1, 128), 1)
    low_end = jnp.zeros((1, 128), jnp.int32)
    high_end = jnp.zeros((1, 128), jnp.int32)
    end = jnp.int32(0)
    for d in range(docs):
        low_end = jnp.where(lane == d, end, low_end)
        end = end + doc_ref[d]
        high_end = jnp.where(lane == d, end, high_end)
    row = lax.broadcasted_iota(jnp.int32, (n_rows, 128), 0)

    def inside(offset):
        pos = row + (me - offset) * n_rows
        return (pos >= low_end) & (pos < high_end)

    qe[...] = jnp.where(inside(0), 1.0, 0.0).astype(jnp.bfloat16).reshape(qe.shape)
    ke[0] = jnp.where(inside(0), 0.0, LOW).astype(jnp.bfloat16)

    for j in range(1, SPAN + 1):

        @pl.when(me < j)
        def _(j=j):
            kvb[j] = jnp.zeros(kvb.shape[1:], kvb.dtype)

    pl.semaphore_wait(barrier, n_friends)

    def start_own(c):
        @if_ahead(1)
        def _():
            up_copy(1, c).start()

    start_own(FAR)

    @if_behind(SPAN + 1)
    def _():
        tell(ready, behind(SPAN + 1))

    for j in range(2, SPAN + 1):

        @pl.when((me >= j) & (me - j + SPAN + 1 > end_ctx))
        def _(j=j):
            tell(ready, behind(j))

    w_copy.start()

    def start_jump(e):
        @if_ahead(SPAN + 1)
        def _():
            if e == 0:
                pl.semaphore_wait(ready, 1)
            jump_copy(e).start()

        @pl.when(me + SPAN + 1 > end_ctx)
        def _():
            if e == 0:

                @if_ahead(2)
                def _():
                    pl.semaphore_wait(ready, jnp.minimum(end_ctx - me, SPAN) - 1)

            for j in range(2, SPAN + 1):

                @if_ahead(j)
                def _(j=j):
                    end_copy(j, e).start()

    for j in range(1, SPAN + 1):
        ke[j] = jnp.where(inside(j), 0.0, LOW).astype(jnp.bfloat16)

    def got_up(j, c):
        @if_behind(j)
        def _():
            up_copy(j, c).wait_recv()
            if j < SPAN and c < FAR:

                @if_ahead(1)
                def _():
                    up_copy(j + 1, c).start()

    def got_jump(e):
        @if_behind(SPAN + 1)
        def _():
            jump_copy(e).wait_recv()
            for j in (2, 3, 4):
                down_copy(j, e).start()

    def got_down(j, e):
        @if_behind(j)
        def _():
            down_copy(j, e).wait_recv()

    scale = math.log2(math.e) / math.sqrt(HEAD_DIM)

    def keys_of(spans):
        k = jnp.concatenate([kvb[j, 0, r : r + n, :] for j, r, n in spans], axis=0)
        e = jnp.concatenate([ke[j, r : r + n, :] for j, r, n in spans], axis=0)
        return jnp.concatenate([k, e], axis=1)

    def values_of(spans):
        v = jnp.concatenate([kvb[j, 1, r : r + n, :] for j, r, n in spans], axis=0)
        return jnp.concatenate([v, jnp.ones_like(v)], axis=1)

    def scores(item):
        t, spans, first = item
        q = jnp.concatenate([qs[t], jnp.concatenate([qe[t]] * heads, axis=0)], axis=1)
        s = lax.dot_general(q, keys_of(spans), (((1,), (1,)), ((), ())), preferred_element_type=jnp.float32)
        if first:
            n = s.shape[1]
            shape = (TILE * heads, TILE)
            key = lax.broadcasted_iota(jnp.int32, shape, 1)
            query = lax.broadcasted_iota(jnp.int32, (heads, TILE, TILE), 1).reshape(shape)
            own = jnp.where(key <= query, s[:, n - TILE :], LOW)
            s = own if n == TILE else jnp.concatenate([s[:, : n - TILE], own], axis=1)
        return s

    def soften(item, s):
        t, _, first = item
        copies = s.shape[1] // 128
        most = jnp.broadcast_to(jnp.max(s, axis=1, keepdims=True), (s.shape[0], 128))
        if first:
            factor = None
        else:
            before = top[t]
            most = jnp.maximum(before, most)
            factor = jnp.exp2((before - most) * scale)
        weights = jnp.exp2((s - jnp.concatenate([most] * copies, axis=1)) * scale).astype(jnp.bfloat16)
        top[t] = most
        return weights, factor

    def gather(item, weights, factor):
        t, spans, first = item
        part = jnp.dot(weights, values_of(spans), preferred_element_type=jnp.float32)
        if first:
            acc[t] = part
        else:
            acc[t] = acc[t] * jnp.concatenate([factor, factor], axis=1) + part

    def attend(items):
        held = scores(items[0])
        pending = None
        for i, item in enumerate(items):
            following = scores(items[i + 1]) if i + 1 < len(items) else None
            now = soften(item, held)
            if pending is not None:
                gather(*pending)
            pending = (item, *now)
            held = following
        gather(*pending)

    kv_copy.wait()
    for c in q_copies:
        c.wait()
    first = [(t, [(0, 0, (t + 1) * TILE)], True) for t in range(n_tiles)]
    attend(first[:2])
    start_own(2)
    attend(first[2:3])
    start_own(1)
    attend(first[3:])
    start_own(0)
    start_jump(0)

    def whole(n, rows):
        return [(t, [(n, 0, rows)], False) for t in range(n_tiles)]

    got_up(1, 3)
    start_jump(1)
    got_up(1, 2)
    got_up(1, 1)
    got_jump(0)
    got_up(1, 0)
    got_jump(1)
    attend(whole(1, n_rows)[:2])
    got_up(2, 2)
    attend(whole(1, n_rows)[2:])
    w_remote.start()
    got_up(2, 1)
    got_up(2, 0)
    attend(whole(2, FAR * TILE)[:2])
    got_up(3, 2)
    attend(whole(2, FAR * TILE)[2:])
    got_up(3, 1)
    got_up(3, 0)
    attend(whole(3, FAR * TILE)[:2])
    attend(whole(3, FAR * TILE)[2:])

    def ends(*blocks):
        for j in blocks:
            for e in range(2):
                got_down(j, e)
        return [(j, FAR * TILE, TILE) for j in blocks]

    spans = ends(4, 3)
    attend([(t, spans, False) for t in range(n_tiles)])
    got_up(4, 2)
    got_up(4, 1)

    def finish(t):
        a = acc[t]
        done = (a[:, :HEAD_DIM] / a[:, HEAD_DIM:]).astype(jnp.bfloat16)
        for h in range(heads):
            att[t, :, h * HEAD_DIM : (h + 1) * HEAD_DIM] = done[h * TILE : (h + 1) * TILE, :]
        att_copy(t).start()

    def att_copy(t):
        return remote(att.at[t], att_sib.at[t], att_send.at[t], att_recv.at[t], (me, sib))

    spans = ends(2)
    starts = {t: max(t, 1) * TILE for t in (3, 2, 1, 0)}
    attend(
        [
            (t, ([(SPAN, r, FAR * TILE - r)] if r < FAR * TILE else []) + spans, False)
            for t, r in starts.items()
        ]
    )
    for t in (3, 2, 1):
        finish(t)
    got_up(4, 0)
    attend([(0, [(SPAN, 0, TILE)], False)])
    finish(0)

    w_copy.wait()
    w_remote.wait()
    sends = []

    def project(place):
        t = (x2, x1, x3, x)[place]
        sides = [slice(side * half_cols, (side + 1) * half_cols) for side in range(2)]
        totals = [jnp.dot(att[t], wbuf[0, :, cols], preferred_element_type=jnp.float32) for cols in sides]
        att_copy(t).wait_recv()
        for side, cols in enumerate(sides):
            total = totals[side] + jnp.dot(att_sib[t], wbuf[1, :, cols], preferred_element_type=jnp.float32)
            pbuf[place, side] = total.astype(jnp.bfloat16)

    def send(copy):
        copy.start()
        sends.append(copy)
        return copy

    rows_out = TILE // 2
    partner = (x1, x3)

    def last_piece(k, side):
        return last_hbm.at[:, pl.ds(pl.multiple_of((2 * k + side) * half_cols, 128), half_cols)]

    def to_cores(src, dst, send_sem, recv_sem, side, chip):
        for k in range(2):
            send(
                remote(
                    src.at[pl.ds(k * rows_out, rows_out), :],
                    dst,
                    send_sem.at[side, k],
                    recv_sem.at[core, side],
                    (me, chip * 2 + k),
                )
            )

    project(0)
    hops = [
        remote(pbuf.at[0, side], step_in.at[side], s1_send.at[side], s1_recv.at[side], (me, partner[side] * 2 + core))
        for side in range(2)
    ]
    for hop in hops:
        hop.start()
    for place in (1, 2, 3):
        project(place)
    to_cores(pbuf.at[1, 0], near.at[core, 0], near_send, near_recv, 0, x1)
    to_cores(pbuf.at[2, 1], near.at[core, 1], near_send, near_recv, 1, x3)
    other = pl.multiple_of((1 - core) * rows_out, rows_out)
    own = pl.multiple_of(core * rows_out, rows_out)
    mine_copy = send(
        remote(pbuf.at[3, :, pl.ds(other, rows_out), :], mine, mine_send, mine_recv, (me, sib))
    )
    for side in range(2):
        hops[side].wait_recv()
        sends.append(hops[side])
        held = pbuf[2 - side, side].astype(jnp.float32) + step_in[side].astype(jnp.float32)
        fwd[side] = held.astype(jnp.bfloat16)
        to_cores(fwd.at[side], last_piece(core, side), last_send, last_recv, side, partner[1 - side])

    def arrived(dst, sems_s, sems_r, k, side):
        remote(near.at[k, side], dst, sems_s.at[side, 0], sems_r.at[k, side], (me, sib)).wait_recv()

    mine_copy.wait_recv()
    for k in range(2):
        for side in range(2):
            arrived(near.at[k, side], near_send, near_recv, k, side)
            here = pbuf[3, side, pl.ds(own, rows_out), :].astype(jnp.float32)
            there = mine[side].astype(jnp.float32)
            base = jnp.where(core == k, here, there)
            col = (2 * k + side) * half_cols
            sums[:, col : col + half_cols] = base + near[k, side].astype(jnp.float32)
    sum_copy = pltpu.make_async_copy(sums, sum_hbm, sum_sem)
    sum_copy.start()
    for k in range(2):
        for side in range(2):
            arrived(last_piece(k, side), last_send, last_recv, k, side)
    sum_copy.wait()

    for copy in sends:
        copy.wait_send()
    for t in range(n_tiles):
        att_copy(t).wait_send()

    @if_ahead(1)
    def _():
        for c in range(FAR + 1):
            up_copy(1, c).wait_send()
        for j in range(2, SPAN + 1):

            @if_behind(j - 1)
            def _(j=j):
                for c in range(FAR):
                    up_copy(j, c).wait_send()

    @if_ahead(SPAN + 1)
    def _():
        for e in range(2):
            jump_copy(e).wait_send()

    @if_behind(SPAN + 1)
    def _():
        for e in range(2):
            for j in (2, 3, 4):
                down_copy(j, e).wait_send()

    @pl.when(me + SPAN + 1 > end_ctx)
    def _():
        for j in range(2, SPAN + 1):

            @if_ahead(j)
            def _(j=j):
                for e in range(2):
                    end_copy(j, e).wait_send()


def on_device(queries, keys_values, doc_lengths, out_weight):
    rows, width = queries.shape
    cols = out_weight.shape[1]
    heads = width // HEAD_DIM
    tiles = rows // TILE
    half = cols // 4
    n_tp = lax.axis_size("tp")
    bf, f32 = jnp.bfloat16, jnp.float32
    dma = pltpu.SemaphoreType.DMA
    hbm = pl.BlockSpec(memory_space=pl.ANY)
    sums, lasts = pl.pallas_call(
        kernel,
        out_shape=[jax.ShapeDtypeStruct((rows // n_tp, cols), kind) for kind in (f32, bf)],
        in_specs=[hbm, hbm, hbm, hbm],
        out_specs=[hbm, hbm],
        scratch_shapes=[
            pltpu.VMEM((tiles, heads * TILE, HEAD_DIM), bf),
            pltpu.VMEM((tiles, TILE, 128), bf),
            pltpu.VMEM((SPAN + 1, rows, 128), bf),
            pltpu.VMEM((SPAN + 1, 2, rows, HEAD_DIM), bf),
            pltpu.VMEM((2, 2, PART, HEAD_DIM), bf),
            pltpu.VMEM((tiles, heads * TILE, 128), f32),
            pltpu.VMEM((tiles, heads * TILE, 2 * HEAD_DIM), f32),
            pltpu.VMEM((tiles, TILE, width), bf),
            pltpu.VMEM((tiles, TILE, width), bf),
            pltpu.VMEM((2, width, cols // 2), bf),
            pltpu.VMEM((tiles, 2, TILE, half), bf),
            pltpu.VMEM((2, TILE, half), bf),
            pltpu.VMEM((2, TILE, half), bf),
            pltpu.VMEM((2, 2, TILE // 2, half), bf),
            pltpu.VMEM((TILE // 2, cols), f32),
            pltpu.VMEM((2, TILE // 2, half), bf),
            pltpu.SMEM(doc_lengths.shape, jnp.int32),
            dma, dma((heads,)), dma, dma, dma,
            dma((SPAN, FAR + 1)), dma((SPAN, FAR + 1)), dma((2,)), dma((2,)), dma((SPAN - 1, 2)), dma((SPAN - 1, 2)), dma((SPAN - 1, 2)), dma, dma, dma((4,)), dma((4,)),
            dma((2,)), dma((2,)), dma((2, 2)), dma((2, 2)), dma((2, 2)), dma((2, 2)), dma, dma,
            pltpu.SemaphoreType.REGULAR,
        ],
        compiler_params=pltpu.CompilerParams(
            collective_id=0, has_side_effects=True, vmem_limit_bytes=40 << 20
        ),
        cost_estimate=pl.CostEstimate(flops=8_000_000_000, bytes_accessed=8_000_000, transcendentals=6_000_000),
        name="attend_project",
    )(
        *(
            pltpu.with_memory_space_constraint(a, pltpu.HBM)
            for a in (doc_lengths, queries.reshape(tiles, TILE, width), keys_values, out_weight)
        )
    )
    return (sums + lasts.astype(f32)).astype(bf)


def solution(mesh):
    placed = (P("ctx", "tp"), P(None, "ctx", "tp"), P(), P("tp", None))
    return jax.shard_map(
        on_device, mesh=mesh, in_specs=placed, out_specs=P(("ctx", "tp"), None), check_vma=False
    )
```

```python
import math

import jax
import jax.numpy as jnp
from jax import lax
from jax.experimental import pallas as pl
from jax.experimental.pallas import tpu as pltpu
from jax.sharding import PartitionSpec as P

HEAD_DIM = 128
SPAN = 4
TILE = 128
LOW = -(2.0**100)
LOGICAL = pl.DeviceIdType.MESH
FAR = 3
PART = TILE // 2


def kernel(
    doc_hbm, q_hbm, kv_hbm, w_hbm, sum_hbm, last_hbm,
    qs, qe, ke, kvb, relay, top, acc, att, att_sib, wbuf, pbuf, step_in, fwd, near, sums, mine, doc_ref,
    doc_sem, q_sem, kv_sem, w_sem, sum_sem,
    up_send, up_recv, jump_send, jump_recv, down_send, down_recv, end_send, w_send, w_recv, att_send, att_recv,
    s1_send, s1_recv, near_send, near_recv, last_send, last_recv, mine_send, mine_recv, ready,
):
    n_ctx = lax.axis_size("ctx")
    n_rows = kvb.shape[2]
    n_tiles = n_rows // TILE
    heads = qs.shape[1] // TILE
    docs = doc_ref.shape[0]
    half_cols = pbuf.shape[3]
    me = lax.axis_index("ctx")
    tp = lax.axis_index("tp")
    x = tp // 2
    core = tp % 2
    x1 = x + 1 - 2 * (x % 2)
    x2 = (x + 2) % 4
    x3 = 3 - x
    end_ctx = n_ctx - 1
    sib = x * 2 + 1 - core

    def ahead(by):
        return jnp.minimum(me + by, end_ctx), tp

    def behind(by):
        return jnp.maximum(me - by, 0), tp

    doc_copy = pltpu.make_async_copy(doc_hbm, doc_ref, doc_sem)
    doc_copy.start()
    barrier = pltpu.get_barrier_semaphore()

    def tell(semaphore, who):
        pl.semaphore_signal(semaphore, inc=1, device_id=who, device_id_type=LOGICAL)

    def if_ahead(by):
        return pl.when(me + by <= end_ctx)

    def if_behind(by):
        return pl.when(me >= by)

    n_friends = 5
    for by in range(1, SPAN + 2):

        @if_ahead(by)
        def _(by=by):
            tell(barrier, ahead(by))

        n_friends = n_friends + jnp.where(me >= by, 1, 0)

    @if_behind(1)
    def _():
        tell(barrier, behind(1))

    n_friends = n_friends + jnp.where(me < end_ctx, 1, 0)
    tell(barrier, (me, sib))
    for chip in (x1, x3):
        for k in range(2):
            tell(barrier, (me, chip * 2 + k))

    q_copies = [
        pltpu.make_async_copy(
            q_hbm.at[:, :, pl.ds(h * HEAD_DIM, HEAD_DIM)],
            qs.at[:, pl.ds(h * TILE, TILE), :],
            q_sem.at[h],
        )
        for h in range(heads)
    ]
    kv_copy = pltpu.make_async_copy(kv_hbm, kvb.at[0], kv_sem)
    my_cols = pl.ds(pl.multiple_of(core * 2 * half_cols, 128), 2 * half_cols)
    sib_cols = pl.ds(pl.multiple_of((1 - core) * 2 * half_cols, 128), 2 * half_cols)
    w_copy = pltpu.make_async_copy(w_hbm.at[:, my_cols], wbuf.at[0], w_sem)
    kv_copy.start()
    for c in q_copies:
        c.start()

    def remote(src, dst, send, recv, to):
        return pltpu.make_async_remote_copy(
            src_ref=src, dst_ref=dst, send_sem=send, recv_sem=recv, device_id=to, device_id_type=LOGICAL
        )

    def piece(ref, c):
        return ref.at[:, pl.ds(c * TILE, TILE), :]

    def up_copy(j, c):
        src = piece(kv_hbm if j == 1 else kvb.at[j - 1], c)
        return remote(src, piece(kvb.at[j], c), up_send.at[j - 1, c], up_recv.at[j - 1, c], ahead(1))

    def part(ref, e):
        return ref.at[:, pl.ds(FAR * TILE + e * PART, PART), :]

    def jump_copy(e):
        return remote(part(kv_hbm, e), relay.at[e], jump_send.at[e], jump_recv.at[e], ahead(SPAN + 1))

    def down_copy(j, e):
        return remote(
            relay.at[e], part(kvb.at[j], e), down_send.at[j - 2, e], down_recv.at[j - 2, e], behind(SPAN + 1 - j)
        )

    def end_copy(j, e):
        return remote(
            part(kv_hbm, e), part(kvb.at[j], e), end_send.at[j - 2, e], down_recv.at[j - 2, e], ahead(j)
        )

    w_remote = remote(w_hbm.at[:, sib_cols], wbuf.at[1], w_send, w_recv, (me, sib))

    pl.semaphore_wait(barrier, n_friends)

    def start_own(c):
        @if_ahead(1)
        def _():
            up_copy(1, c).start()

    start_own(FAR)

    @if_behind(SPAN + 1)
    def _():
        tell(ready, behind(SPAN + 1))

    for j in range(2, SPAN + 1):

        @pl.when((me >= j) & (me - j + SPAN + 1 > end_ctx))
        def _(j=j):
            tell(ready, behind(j))

    w_copy.start()

    doc_copy.wait()
    lane = lax.broadcasted_iota(jnp.int32, (1, 128), 1)
    low_end = jnp.zeros((1, 128), jnp.int32)
    high_end = jnp.zeros((1, 128), jnp.int32)
    end = jnp.int32(0)
    for d in range(docs):
        low_end = jnp.where(lane == d, end, low_end)
        end = end + doc_ref[d]
        high_end = jnp.where(lane == d, end, high_end)
    row = lax.broadcasted_iota(jnp.int32, (n_rows, 128), 0)

    def inside(offset):
        pos = row + (me - offset) * n_rows
        return (pos >= low_end) & (pos < high_end)

    qe[...] = jnp.where(inside(0), 1.0, 0.0).astype(jnp.bfloat16).reshape(qe.shape)
    ke[0] = jnp.where(inside(0), 0.0, LOW).astype(jnp.bfloat16)

    for j in range(1, SPAN + 1):

        @pl.when(me < j)
        def _(j=j):
            kvb[j] = jnp.zeros(kvb.shape[1:], kvb.dtype)

    start_own(2)

    def start_jump(e):
        @if_ahead(SPAN + 1)
        def _():
            if e == 0:
                pl.semaphore_wait(ready, 1)
            jump_copy(e).start()

        @pl.when(me + SPAN + 1 > end_ctx)
        def _():
            if e == 0:

                @if_ahead(2)
                def _():
                    pl.semaphore_wait(ready, jnp.minimum(end_ctx - me, SPAN) - 1)

            for j in range(2, SPAN + 1):

                @if_ahead(j)
                def _(j=j):
                    end_copy(j, e).start()

    for j in range(1, SPAN + 1):
        ke[j] = jnp.where(inside(j), 0.0, LOW).astype(jnp.bfloat16)

    def got_up(j, c):
        @if_behind(j)
        def _():
            up_copy(j, c).wait_recv()
            if j < SPAN and c < FAR:

                @if_ahead(1)
                def _():
                    up_copy(j + 1, c).start()

    def got_jump(e):
        @if_behind(SPAN + 1)
        def _():
            jump_copy(e).wait_recv()
            for j in (2, 3, 4):
                down_copy(j, e).start()

    def got_down(j, e):
        @if_behind(j)
        def _():
            down_copy(j, e).wait_recv()

    scale = math.log2(math.e) / math.sqrt(HEAD_DIM)

    def keys_of(spans):
        k = jnp.concatenate([kvb[j, 0, r : r + n, :] for j, r, n in spans], axis=0)
        e = jnp.concatenate([ke[j, r : r + n, :] for j, r, n in spans], axis=0)
        return jnp.concatenate([k, e], axis=1)

    def values_of(spans):
        v = jnp.concatenate([kvb[j, 1, r : r + n, :] for j, r, n in spans], axis=0)
        return jnp.concatenate([v, jnp.ones_like(v)], axis=1)

    def scores(item):
        t, spans, first = item
        q = jnp.concatenate([qs[t], jnp.concatenate([qe[t]] * heads, axis=0)], axis=1)
        s = lax.dot_general(q, keys_of(spans), (((1,), (1,)), ((), ())), preferred_element_type=jnp.float32)
        if first:
            n = s.shape[1]
            shape = (TILE * heads, TILE)
            key = lax.broadcasted_iota(jnp.int32, shape, 1)
            query = lax.broadcasted_iota(jnp.int32, (heads, TILE, TILE), 1).reshape(shape)
            own = jnp.where(key <= query, s[:, n - TILE :], LOW)
            s = own if n == TILE else jnp.concatenate([s[:, : n - TILE], own], axis=1)
        return s

    def soften(item, s):
        t, _, first = item
        copies = s.shape[1] // 128
        most = jnp.broadcast_to(jnp.max(s, axis=1, keepdims=True), (s.shape[0], 128))
        if first:
            factor = None
        else:
            before = top[t]
            most = jnp.maximum(before, most)
            factor = jnp.exp2((before - most) * scale)
        weights = jnp.exp2((s - jnp.concatenate([most] * copies, axis=1)) * scale).astype(jnp.bfloat16)
        top[t] = most
        return weights, factor

    def gather(item, weights, factor):
        t, spans, first = item
        part = jnp.dot(weights, values_of(spans), preferred_element_type=jnp.float32)
        if first:
            acc[t] = part
        else:
            acc[t] = acc[t] * jnp.concatenate([factor, factor], axis=1) + part

    def attend(items, then=None):
        held = scores(items[0])
        pending = None
        for i, item in enumerate(items):
            following = scores(items[i + 1]) if i + 1 < len(items) else None
            now = soften(item, held)
            if pending is not None:
                gather(*pending)
                if then is not None:
                    then(pending[0][0])
            pending = (item, *now)
            held = following
        gather(*pending)
        if then is not None:
            then(pending[0][0])

    kv_copy.wait()
    for c in q_copies:
        c.wait()
    first = [(t, [(0, 0, (t + 1) * TILE)], True) for t in range(n_tiles)]
    start_own(1)
    attend(first[:2])
    start_own(0)
    attend(first[2:])
    start_jump(0)

    def whole(n, rows):
        return [(t, [(n, 0, rows)], False) for t in range(n_tiles)]

    got_up(1, 3)
    start_jump(1)
    got_up(1, 2)
    got_up(1, 1)
    got_jump(0)
    got_up(1, 0)
    got_jump(1)
    attend(whole(1, n_rows)[:2])
    got_up(2, 2)
    attend(whole(1, n_rows)[2:])
    w_remote.start()
    got_up(2, 1)
    got_up(2, 0)
    attend(whole(2, FAR * TILE)[:2])
    got_up(3, 2)
    attend(whole(2, FAR * TILE)[2:])
    got_up(3, 1)
    got_up(3, 0)
    attend(whole(3, FAR * TILE)[:2])
    attend(whole(3, FAR * TILE)[2:])

    def ends(*blocks):
        for j in blocks:
            for e in range(2):
                got_down(j, e)
        return [(j, FAR * TILE, TILE) for j in blocks]

    spans = ends(4, 3)
    got_up(4, 2)
    attend([(t, ([(SPAN, 2 * TILE, TILE)] if t < 3 else []) + spans, False) for t in range(n_tiles)])
    got_up(4, 1)
    got_up(4, 0)

    def finish(t):
        a = acc[t]
        done = (a[:, :HEAD_DIM] / a[:, HEAD_DIM:]).astype(jnp.bfloat16)
        for h in range(heads):
            att[t, :, h * HEAD_DIM : (h + 1) * HEAD_DIM] = done[h * TILE : (h + 1) * TILE, :]
        att_copy(t).start()

    def att_copy(t):
        return remote(att.at[t], att_sib.at[t], att_send.at[t], att_recv.at[t], (me, sib))

    spans = ends(2)
    attend(
        [(t, ([(SPAN, t * TILE, (2 - t) * TILE)] if t < 2 else []) + spans, False) for t in range(n_tiles)],
        finish,
    )

    w_copy.wait()
    w_remote.wait()
    sends = []

    def project(place):
        t = (x2, x1, x3, x)[place]
        sides = [slice(side * half_cols, (side + 1) * half_cols) for side in range(2)]
        totals = [jnp.dot(att[t], wbuf[0, :, cols], preferred_element_type=jnp.float32) for cols in sides]
        att_copy(t).wait_recv()
        for side, cols in enumerate(sides):
            total = totals[side] + jnp.dot(att_sib[t], wbuf[1, :, cols], preferred_element_type=jnp.float32)
            pbuf[place, side] = total.astype(jnp.bfloat16)

    def send(copy):
        copy.start()
        sends.append(copy)
        return copy

    rows_out = TILE // 2
    partner = (x1, x3)

    def last_piece(k, side):
        return last_hbm.at[:, pl.ds(pl.multiple_of((2 * k + side) * half_cols, 128), half_cols)]

    def to_core(src, dst, send_sem, recv_sem, side, chip, k):
        send(
            remote(
                src.at[pl.ds(k * rows_out, rows_out), :],
                dst,
                send_sem.at[side, k],
                recv_sem.at[core, side],
                (me, chip * 2 + k),
            )
        )

    def hop(side, k):
        rows_k = pl.ds(k * rows_out, rows_out)
        return remote(
            pbuf.at[0, side, rows_k, :],
            step_in.at[side, rows_k, :],
            s1_send.at[side, k],
            s1_recv.at[side, k],
            (me, partner[side] * 2 + core),
        )

    for place, k in enumerate((1, 0)):
        project(place)
        for side in range(2):
            send(hop(side, k))
    project(2)
    project(3)
    other = pl.multiple_of((1 - core) * rows_out, rows_out)
    own = pl.multiple_of(core * rows_out, rows_out)
    mine_copy = send(
        remote(pbuf.at[3, :, pl.ds(other, rows_out), :], mine, mine_send, mine_recv, (me, sib))
    )
    for half in (1,):
        to_core(pbuf.at[1, 0], near.at[core, 0], near_send, near_recv, 0, x1, half)
        to_core(pbuf.at[2, 1], near.at[core, 1], near_send, near_recv, 1, x3, half)
    for k in (1, 0):
        rows_k = slice(k * rows_out, (k + 1) * rows_out)
        for side in range(2):
            hop(side, k).wait_recv()
            held = pbuf[2 - side, side, rows_k, :].astype(jnp.float32) + step_in[side, rows_k, :].astype(jnp.float32)
            fwd[side, rows_k, :] = held.astype(jnp.bfloat16)
            to_core(fwd.at[side], last_piece(core, side), last_send, last_recv, side, partner[1 - side], k)
        if k == 1:
            for half in (0,):
                to_core(pbuf.at[1, 0], near.at[core, 0], near_send, near_recv, 0, x1, half)
                to_core(pbuf.at[2, 1], near.at[core, 1], near_send, near_recv, 1, x3, half)

    def arrived(dst, sems_s, sems_r, k, side):
        remote(near.at[k, side], dst, sems_s.at[side, 0], sems_r.at[k, side], (me, sib)).wait_recv()

    mine_copy.wait_recv()
    for k in range(2):
        for side in range(2):
            arrived(near.at[k, side], near_send, near_recv, k, side)
            here = pbuf[3, side, pl.ds(own, rows_out), :].astype(jnp.float32)
            there = mine[side].astype(jnp.float32)
            base = jnp.where(core == k, here, there)
            col = (2 * k + side) * half_cols
            sums[:, col : col + half_cols] = base + near[k, side].astype(jnp.float32)
    sum_copy = pltpu.make_async_copy(sums, sum_hbm, sum_sem)
    sum_copy.start()
    for k in range(2):
        for side in range(2):
            arrived(last_piece(k, side), last_send, last_recv, k, side)
    sum_copy.wait()

    for copy in sends:
        copy.wait_send()
    for t in range(n_tiles):
        att_copy(t).wait_send()

    @if_ahead(1)
    def _():
        for c in range(FAR + 1):
            up_copy(1, c).wait_send()
        for j in range(2, SPAN + 1):

            @if_behind(j - 1)
            def _(j=j):
                for c in range(FAR):
                    up_copy(j, c).wait_send()

    @if_ahead(SPAN + 1)
    def _():
        for e in range(2):
            jump_copy(e).wait_send()

    @if_behind(SPAN + 1)
    def _():
        for e in range(2):
            for j in (2, 3, 4):
                down_copy(j, e).wait_send()

    @pl.when(me + SPAN + 1 > end_ctx)
    def _():
        for j in range(2, SPAN + 1):

            @if_ahead(j)
            def _(j=j):
                for e in range(2):
                    end_copy(j, e).wait_send()


def on_device(queries, keys_values, doc_lengths, out_weight):
    rows, width = queries.shape
    cols = out_weight.shape[1]
    heads = width // HEAD_DIM
    tiles = rows // TILE
    half = cols // 4
    n_tp = lax.axis_size("tp")
    bf, f32 = jnp.bfloat16, jnp.float32
    dma = pltpu.SemaphoreType.DMA
    hbm = pl.BlockSpec(memory_space=pl.ANY)
    sums, lasts = pl.pallas_call(
        kernel,
        out_shape=[jax.ShapeDtypeStruct((rows // n_tp, cols), kind) for kind in (f32, bf)],
        in_specs=[hbm, hbm, hbm, hbm],
        out_specs=[hbm, hbm],
        scratch_shapes=[
            pltpu.VMEM((tiles, heads * TILE, HEAD_DIM), bf),
            pltpu.VMEM((tiles, TILE, 128), bf),
            pltpu.VMEM((SPAN + 1, rows, 128), bf),
            pltpu.VMEM((SPAN + 1, 2, rows, HEAD_DIM), bf),
            pltpu.VMEM((2, 2, PART, HEAD_DIM), bf),
            pltpu.VMEM((tiles, heads * TILE, 128), f32),
            pltpu.VMEM((tiles, heads * TILE, 2 * HEAD_DIM), f32),
            pltpu.VMEM((tiles, TILE, width), bf),
            pltpu.VMEM((tiles, TILE, width), bf),
            pltpu.VMEM((2, width, cols // 2), bf),
            pltpu.VMEM((tiles, 2, TILE, half), bf),
            pltpu.VMEM((2, TILE, half), bf),
            pltpu.VMEM((2, TILE, half), bf),
            pltpu.VMEM((2, 2, TILE // 2, half), bf),
            pltpu.VMEM((TILE // 2, cols), f32),
            pltpu.VMEM((2, TILE // 2, half), bf),
            pltpu.SMEM(doc_lengths.shape, jnp.int32),
            dma, dma((heads,)), dma, dma, dma,
            dma((SPAN, FAR + 1)), dma((SPAN, FAR + 1)), dma((2,)), dma((2,)), dma((SPAN - 1, 2)), dma((SPAN - 1, 2)), dma((SPAN - 1, 2)), dma, dma, dma((4,)), dma((4,)),
            dma((2, 2)), dma((2, 2)), dma((2, 2)), dma((2, 2)), dma((2, 2)), dma((2, 2)), dma, dma,
            pltpu.SemaphoreType.REGULAR,
        ],
        compiler_params=pltpu.CompilerParams(
            collective_id=0, has_side_effects=True, vmem_limit_bytes=40 << 20
        ),
        cost_estimate=pl.CostEstimate(flops=8_000_000_000, bytes_accessed=8_000_000, transcendentals=6_000_000),
        name="attend_project",
    )(
        *(
            pltpu.with_memory_space_constraint(a, pltpu.HBM)
            for a in (doc_lengths, queries.reshape(tiles, TILE, width), keys_values, out_weight)
        )
    )
    return (sums + lasts.astype(f32)).astype(bf)


def solution(mesh):
    placed = (P("ctx", "tp"), P(None, "ctx", "tp"), P(), P("tp", None))
    return jax.shard_map(
        on_device, mesh=mesh, in_specs=placed, out_specs=P(("ctx", "tp"), None), check_vma=False
    )
```

```python
import math

import jax
import jax.numpy as jnp
from jax import lax
from jax.experimental import pallas as pl
from jax.experimental.pallas import tpu as pltpu
from jax.sharding import PartitionSpec as P

HEAD_DIM = 128
SPAN = 4
TILE = 128
LOW = -(2.0**100)
LOGICAL = pl.DeviceIdType.MESH
FAR = 3
PART = TILE // 2


def kernel(
    doc_hbm, q_hbm, kv_hbm, w_hbm, sum_hbm, last_hbm,
    qs, qe, ke, kvb, relay, top, acc, att, att_sib, wbuf, pbuf, step_in, fwd, near, sums, mine, doc_ref,
    doc_sem, q_sem, kv_sem, w_sem, sum_sem,
    up_send, up_recv, jump_send, jump_recv, down_send, down_recv, end_send, w_send, w_recv, att_send, att_recv,
    s1_send, s1_recv, near_send, near_recv, last_send, last_recv, mine_send, mine_recv, ready,
):
    n_ctx = lax.axis_size("ctx")
    n_rows = kvb.shape[2]
    n_tiles = n_rows // TILE
    heads = qs.shape[1] // TILE
    docs = doc_ref.shape[0]
    half_cols = pbuf.shape[3]
    me = lax.axis_index("ctx")
    tp = lax.axis_index("tp")
    x = tp // 2
    core = tp % 2
    x1 = x + 1 - 2 * (x % 2)
    x2 = (x + 2) % 4
    x3 = 3 - x
    end_ctx = n_ctx - 1
    sib = x * 2 + 1 - core

    def ahead(by):
        return jnp.minimum(me + by, end_ctx), tp

    def behind(by):
        return jnp.maximum(me - by, 0), tp

    doc_copy = pltpu.make_async_copy(doc_hbm, doc_ref, doc_sem)
    doc_copy.start()
    barrier = pltpu.get_barrier_semaphore()

    def tell(semaphore, who):
        pl.semaphore_signal(semaphore, inc=1, device_id=who, device_id_type=LOGICAL)

    def if_ahead(by):
        return pl.when(me + by <= end_ctx)

    def if_behind(by):
        return pl.when(me >= by)

    n_friends = 5
    for by in range(1, SPAN + 2):

        @if_ahead(by)
        def _(by=by):
            tell(barrier, ahead(by))

        n_friends = n_friends + jnp.where(me >= by, 1, 0)

    @if_behind(1)
    def _():
        tell(barrier, behind(1))

    n_friends = n_friends + jnp.where(me < end_ctx, 1, 0)
    tell(barrier, (me, sib))
    for chip in (x1, x3):
        for k in range(2):
            tell(barrier, (me, chip * 2 + k))

    q_copies = [
        pltpu.make_async_copy(
            q_hbm.at[:, :, pl.ds(h * HEAD_DIM, HEAD_DIM)],
            qs.at[:, pl.ds(h * TILE, TILE), :],
            q_sem.at[h],
        )
        for h in range(heads)
    ]
    kv_copy = pltpu.make_async_copy(kv_hbm, kvb.at[0], kv_sem)
    my_cols = pl.ds(pl.multiple_of(core * 2 * half_cols, 128), 2 * half_cols)
    sib_cols = pl.ds(pl.multiple_of((1 - core) * 2 * half_cols, 128), 2 * half_cols)
    w_copy = pltpu.make_async_copy(w_hbm.at[:, my_cols], wbuf.at[0], w_sem)
    kv_copy.start()
    for c in q_copies:
        c.start()

    def remote(src, dst, send, recv, to):
        return pltpu.make_async_remote_copy(
            src_ref=src, dst_ref=dst, send_sem=send, recv_sem=recv, device_id=to, device_id_type=LOGICAL
        )

    def piece(ref, c):
        return ref.at[:, pl.ds(c * TILE, TILE), :]

    def up_copy(j, c):
        src = piece(kv_hbm if j == 1 else kvb.at[j - 1], c)
        return remote(src, piece(kvb.at[j], c), up_send.at[j - 1, c], up_recv.at[j - 1, c], ahead(1))

    def part(ref, e):
        return ref.at[:, pl.ds(FAR * TILE + e * PART, PART), :]

    def jump_copy(e):
        return remote(part(kv_hbm, e), relay.at[e], jump_send.at[e], jump_recv.at[e], ahead(SPAN + 1))

    def down_copy(j, e):
        return remote(
            relay.at[e], part(kvb.at[j], e), down_send.at[j - 2, e], down_recv.at[j - 2, e], behind(SPAN + 1 - j)
        )

    def end_copy(j, e):
        return remote(
            part(kv_hbm, e), part(kvb.at[j], e), end_send.at[j - 2, e], down_recv.at[j - 2, e], ahead(j)
        )

    w_remote = remote(w_hbm.at[:, sib_cols], wbuf.at[1], w_send, w_recv, (me, sib))

    pl.semaphore_wait(barrier, n_friends)

    def start_own(c):
        @if_ahead(1)
        def _():
            up_copy(1, c).start()

    start_own(FAR)

    @if_behind(SPAN + 1)
    def _():
        tell(ready, behind(SPAN + 1))

    for j in range(2, SPAN + 1):

        @pl.when((me >= j) & (me - j + SPAN + 1 > end_ctx))
        def _(j=j):
            tell(ready, behind(j))

    w_copy.start()

    doc_copy.wait()
    lane = lax.broadcasted_iota(jnp.int32, (1, 128), 1)
    low_end = jnp.zeros((1, 128), jnp.int32)
    high_end = jnp.zeros((1, 128), jnp.int32)
    end = jnp.int32(0)
    for d in range(docs):
        low_end = jnp.where(lane == d, end, low_end)
        end = end + doc_ref[d]
        high_end = jnp.where(lane == d, end, high_end)
    row = lax.broadcasted_iota(jnp.int32, (n_rows, 128), 0)

    def inside(offset):
        pos = row + (me - offset) * n_rows
        return (pos >= low_end) & (pos < high_end)

    qe[...] = jnp.where(inside(0), 1.0, 0.0).astype(jnp.bfloat16).reshape(qe.shape)
    ke[0] = jnp.where(inside(0), 0.0, LOW).astype(jnp.bfloat16)

    for j in range(1, SPAN + 1):

        @pl.when(me < j)
        def _(j=j):
            kvb[j] = jnp.zeros(kvb.shape[1:], kvb.dtype)

    start_own(2)

    def start_jump(e):
        @if_ahead(SPAN + 1)
        def _():
            if e == 0:
                pl.semaphore_wait(ready, 1)
            jump_copy(e).start()

        @pl.when(me + SPAN + 1 > end_ctx)
        def _():
            if e == 0:

                @if_ahead(2)
                def _():
                    pl.semaphore_wait(ready, jnp.minimum(end_ctx - me, SPAN) - 1)

            for j in range(2, SPAN + 1):

                @if_ahead(j)
                def _(j=j):
                    end_copy(j, e).start()

    for j in range(1, SPAN + 1):
        ke[j] = jnp.where(inside(j), 0.0, LOW).astype(jnp.bfloat16)

    def got_up(j, c):
        @if_behind(j)
        def _():
            up_copy(j, c).wait_recv()
            if j < SPAN and c < FAR:

                @if_ahead(1)
                def _():
                    up_copy(j + 1, c).start()

    def got_jump(e):
        @if_behind(SPAN + 1)
        def _():
            jump_copy(e).wait_recv()
            for j in (2, 3, 4):
                down_copy(j, e).start()

    def got_down(j, e):
        @if_behind(j)
        def _():
            down_copy(j, e).wait_recv()

    scale = math.log2(math.e) / math.sqrt(HEAD_DIM)

    def keys_of(spans):
        k = jnp.concatenate([kvb[j, 0, r : r + n, :] for j, r, n in spans], axis=0)
        e = jnp.concatenate([ke[j, r : r + n, :] for j, r, n in spans], axis=0)
        return jnp.concatenate([k, e], axis=1)

    def values_of(spans):
        v = jnp.concatenate([kvb[j, 1, r : r + n, :] for j, r, n in spans], axis=0)
        return jnp.concatenate([v, jnp.ones_like(v)], axis=1)

    def scores(item):
        t, spans, first = item
        q = jnp.concatenate([qs[t], jnp.concatenate([qe[t]] * heads, axis=0)], axis=1)
        s = lax.dot_general(q, keys_of(spans), (((1,), (1,)), ((), ())), preferred_element_type=jnp.float32)
        if first:
            n = s.shape[1]
            shape = (TILE * heads, TILE)
            key = lax.broadcasted_iota(jnp.int32, shape, 1)
            query = lax.broadcasted_iota(jnp.int32, (heads, TILE, TILE), 1).reshape(shape)
            own = jnp.where(key <= query, s[:, n - TILE :], LOW)
            s = own if n == TILE else jnp.concatenate([s[:, : n - TILE], own], axis=1)
        return s

    def soften(item, s):
        t, _, first = item
        copies = s.shape[1] // 128
        most = jnp.broadcast_to(jnp.max(s, axis=1, keepdims=True), (s.shape[0], 128))
        if first:
            factor = None
        else:
            before = top[t]
            most = jnp.maximum(before, most)
            factor = jnp.exp2((before - most) * scale)
        weights = jnp.exp2((s - jnp.concatenate([most] * copies, axis=1)) * scale).astype(jnp.bfloat16)
        top[t] = most
        return weights, factor

    def gather(item, weights, factor):
        t, spans, first = item
        part = jnp.dot(weights, values_of(spans), preferred_element_type=jnp.float32)
        if first:
            acc[t] = part
        else:
            acc[t] = acc[t] * jnp.concatenate([factor, factor], axis=1) + part

    def attend(items, then=None):
        held = scores(items[0])
        pending = None
        for i, item in enumerate(items):
            following = scores(items[i + 1]) if i + 1 < len(items) else None
            now = soften(item, held)
            if pending is not None:
                gather(*pending)
                if then is not None:
                    then(pending[0][0])
            pending = (item, *now)
            held = following
        gather(*pending)
        if then is not None:
            then(pending[0][0])

    kv_copy.wait()
    for c in q_copies:
        c.wait()
    first = [(t, [(0, 0, (t + 1) * TILE)], True) for t in range(n_tiles)]
    start_own(1)
    attend(first[:2])
    start_own(0)
    attend(first[2:])
    start_jump(0)

    def whole(n, rows):
        return [(t, [(n, 0, rows)], False) for t in range(n_tiles)]

    got_up(1, 3)
    start_jump(1)
    got_up(1, 2)
    got_up(1, 1)
    got_jump(0)
    got_up(1, 0)
    got_jump(1)
    attend(whole(1, n_rows)[:2])
    got_up(2, 2)
    attend(whole(1, n_rows)[2:])
    w_remote.start()
    got_up(2, 1)
    got_up(2, 0)
    attend(whole(2, FAR * TILE)[:2])
    got_up(3, 2)
    attend(whole(2, FAR * TILE)[2:])
    got_up(3, 1)
    got_up(3, 0)
    attend(whole(3, FAR * TILE)[:2])
    attend(whole(3, FAR * TILE)[2:])

    def ends(*blocks):
        for j in blocks:
            for e in range(2):
                got_down(j, e)
        return [(j, FAR * TILE, TILE) for j in blocks]

    spans = ends(4, 3)
    got_up(4, 2)
    attend([(t, ([(SPAN, 2 * TILE, TILE)] if t < 3 else []) + spans, False) for t in range(n_tiles)])
    got_up(4, 1)
    got_up(4, 0)

    def finish(t):
        a = acc[t]
        done = (a[:, :HEAD_DIM] / a[:, HEAD_DIM:]).astype(jnp.bfloat16)
        for h in range(heads):
            att[t, :, h * HEAD_DIM : (h + 1) * HEAD_DIM] = done[h * TILE : (h + 1) * TILE, :]
        att_copy(t).start()

    def att_copy(t):
        return remote(att.at[t], att_sib.at[t], att_send.at[t], att_recv.at[t], (me, sib))

    spans = ends(2)
    attend(
        [(t, ([(SPAN, t * TILE, (2 - t) * TILE)] if t < 2 else []) + spans, False) for t in range(n_tiles)],
        finish,
    )

    w_copy.wait()
    w_remote.wait()
    sends = []

    def project(place):
        t = (x2, x1, x3, x)[place]
        sides = [slice(side * half_cols, (side + 1) * half_cols) for side in range(2)]
        totals = [jnp.dot(att[t], wbuf[0, :, cols], preferred_element_type=jnp.float32) for cols in sides]
        att_copy(t).wait_recv()
        for side, cols in enumerate(sides):
            total = totals[side] + jnp.dot(att_sib[t], wbuf[1, :, cols], preferred_element_type=jnp.float32)
            pbuf[place, side] = total.astype(jnp.bfloat16)

    def send(copy):
        copy.start()
        sends.append(copy)
        return copy

    rows_out = TILE // 2
    partner = (x1, x3)

    def last_piece(k, side):
        return last_hbm.at[:, pl.ds(pl.multiple_of((2 * k + side) * half_cols, 128), half_cols)]

    def to_core(src, dst, send_sem, recv_sem, side, chip, k):
        send(
            remote(
                src.at[pl.ds(k * rows_out, rows_out), :],
                dst,
                send_sem.at[side, k],
                recv_sem.at[core, side],
                (me, chip * 2 + k),
            )
        )

    def hop(side, k):
        rows_k = pl.ds(k * rows_out, rows_out)
        return remote(
            pbuf.at[0, side, rows_k, :],
            step_in.at[side, rows_k, :],
            s1_send.at[side, k],
            s1_recv.at[side, k],
            (me, partner[side] * 2 + core),
        )

    project(0)
    for k in range(2):
        for side in range(2):
            send(hop(side, k))
    project(1)
    project(2)
    project(3)
    other = pl.multiple_of((1 - core) * rows_out, rows_out)
    own = pl.multiple_of(core * rows_out, rows_out)
    mine_copy = send(
        remote(pbuf.at[3, :, pl.ds(other, rows_out), :], mine, mine_send, mine_recv, (me, sib))
    )
    for half in (1, 0):
        to_core(pbuf.at[1, 0], near.at[core, 0], near_send, near_recv, 0, x1, half)
        to_core(pbuf.at[2, 1], near.at[core, 1], near_send, near_recv, 1, x3, half)
    for k in (1, 0):
        rows_k = slice(k * rows_out, (k + 1) * rows_out)
        for side in range(2):
            hop(side, k).wait_recv()
            held = pbuf[2 - side, side, rows_k, :].astype(jnp.float32) + step_in[side, rows_k, :].astype(jnp.float32)
            fwd[side, rows_k, :] = held.astype(jnp.bfloat16)
            to_core(fwd.at[side], last_piece(core, side), last_send, last_recv, side, partner[1 - side], k)

    def arrived(dst, sems_s, sems_r, k, side):
        remote(near.at[k, side], dst, sems_s.at[side, 0], sems_r.at[k, side], (me, sib)).wait_recv()

    mine_copy.wait_recv()
    for k in range(2):
        for side in range(2):
            arrived(near.at[k, side], near_send, near_recv, k, side)
            here = pbuf[3, side, pl.ds(own, rows_out), :].astype(jnp.float32)
            there = mine[side].astype(jnp.float32)
            base = jnp.where(core == k, here, there)
            col = (2 * k + side) * half_cols
            sums[:, col : col + half_cols] = base + near[k, side].astype(jnp.float32)
    sum_copy = pltpu.make_async_copy(sums, sum_hbm, sum_sem)
    sum_copy.start()
    for k in range(2):
        for side in range(2):
            arrived(last_piece(k, side), last_send, last_recv, k, side)
    sum_copy.wait()

    for copy in sends:
        copy.wait_send()
    for t in range(n_tiles):
        att_copy(t).wait_send()

    @if_ahead(1)
    def _():
        for c in range(FAR + 1):
            up_copy(1, c).wait_send()
        for j in range(2, SPAN + 1):

            @if_behind(j - 1)
            def _(j=j):
                for c in range(FAR):
                    up_copy(j, c).wait_send()

    @if_ahead(SPAN + 1)
    def _():
        for e in range(2):
            jump_copy(e).wait_send()

    @if_behind(SPAN + 1)
    def _():
        for e in range(2):
            for j in (2, 3, 4):
                down_copy(j, e).wait_send()

    @pl.when(me + SPAN + 1 > end_ctx)
    def _():
        for j in range(2, SPAN + 1):

            @if_ahead(j)
            def _(j=j):
                for e in range(2):
                    end_copy(j, e).wait_send()


def on_device(queries, keys_values, doc_lengths, out_weight):
    rows, width = queries.shape
    cols = out_weight.shape[1]
    heads = width // HEAD_DIM
    tiles = rows // TILE
    half = cols // 4
    n_tp = lax.axis_size("tp")
    bf, f32 = jnp.bfloat16, jnp.float32
    dma = pltpu.SemaphoreType.DMA
    hbm = pl.BlockSpec(memory_space=pl.ANY)
    sums, lasts = pl.pallas_call(
        kernel,
        out_shape=[jax.ShapeDtypeStruct((rows // n_tp, cols), kind) for kind in (f32, bf)],
        in_specs=[hbm, hbm, hbm, hbm],
        out_specs=[hbm, hbm],
        scratch_shapes=[
            pltpu.VMEM((tiles, heads * TILE, HEAD_DIM), bf),
            pltpu.VMEM((tiles, TILE, 128), bf),
            pltpu.VMEM((SPAN + 1, rows, 128), bf),
            pltpu.VMEM((SPAN + 1, 2, rows, HEAD_DIM), bf),
            pltpu.VMEM((2, 2, PART, HEAD_DIM), bf),
            pltpu.VMEM((tiles, heads * TILE, 128), f32),
            pltpu.VMEM((tiles, heads * TILE, 2 * HEAD_DIM), f32),
            pltpu.VMEM((tiles, TILE, width), bf),
            pltpu.VMEM((tiles, TILE, width), bf),
            pltpu.VMEM((2, width, cols // 2), bf),
            pltpu.VMEM((tiles, 2, TILE, half), bf),
            pltpu.VMEM((2, TILE, half), bf),
            pltpu.VMEM((2, TILE, half), bf),
            pltpu.VMEM((2, 2, TILE // 2, half), bf),
            pltpu.VMEM((TILE // 2, cols), f32),
            pltpu.VMEM((2, TILE // 2, half), bf),
            pltpu.SMEM(doc_lengths.shape, jnp.int32),
            dma, dma((heads,)), dma, dma, dma,
            dma((SPAN, FAR + 1)), dma((SPAN, FAR + 1)), dma((2,)), dma((2,)), dma((SPAN - 1, 2)), dma((SPAN - 1, 2)), dma((SPAN - 1, 2)), dma, dma, dma((4,)), dma((4,)),
            dma((2, 2)), dma((2, 2)), dma((2, 2)), dma((2, 2)), dma((2, 2)), dma((2, 2)), dma, dma,
            pltpu.SemaphoreType.REGULAR,
        ],
        compiler_params=pltpu.CompilerParams(
            collective_id=0, has_side_effects=True, vmem_limit_bytes=40 << 20
        ),
        cost_estimate=pl.CostEstimate(flops=8_000_000_000, bytes_accessed=8_000_000, transcendentals=6_000_000),
        name="attend_project",
    )(
        *(
            pltpu.with_memory_space_constraint(a, pltpu.HBM)
            for a in (doc_lengths, queries.reshape(tiles, TILE, width), keys_values, out_weight)
        )
    )
    return (sums + lasts.astype(f32)).astype(bf)


def solution(mesh):
    placed = (P("ctx", "tp"), P(None, "ctx", "tp"), P(), P("tp", None))
    return jax.shard_map(
        on_device, mesh=mesh, in_specs=placed, out_specs=P(("ctx", "tp"), None), check_vma=False
    )
```
